256 devices in a mesh: ctx: 16 (over x, y_hi, core), tp: 16 (over y_lo, z).
Axes of the slice: x: 4, y: 4 (y_hi: 2, y_lo: 2; y = y_hi * 2 + y_lo), z: 8, core: 2. Of those that a mesh axis runs over, the one named last changes fastest.
Arguments:
- c_query: bfloat16 [4096, 1536], P('ctx'), may hold values from -6 to 6
- w_uq: bfloat16 [1536, 12288], P(None, 'tp'), may hold values from -0.15625 to 0.15625
- w_uk: bfloat16 [64, 128, 512], P('tp'), may hold values from -0.5 to 0.5
- w_uv: bfloat16 [64, 512, 128], P('tp'), may hold values from -0.25 to 0.25
- w_out: bfloat16 [8192, 7168], P('tp'), may hold values from -0.09375 to 0.09375
- kv_latent: bfloat16 [4096, 576], P('ctx'), may hold values from -48 to 48
- slab_order: int32 [32], replicated, may hold values from 0 to 31, each once
- block_table: int32 [32, 32], replicated, may hold values from 0 to 1, as said below
Outputs:
- attn_out: bfloat16 [4096, 7168], P('ctx', 'tp')
The draws below stay inside these ranges and needn't reach their ends.
Inputs may be any that keep to these rules, and one draw needn't show every extreme that they name: `slab_order`: each of the 32 slabs appears once. `block_table`: entries are 0 or 1, the diagonal is 1.
All inputs are finite; a program needn't handle non-finite values.
Results may differ from the reference program's by a relative error of at most 0.025.
Values may be sent and summed in bfloat16 or wider, within the bound.
A program may use at most 128 MiB of HBM per device.

```python
import jax
import jax.numpy as jnp
from jax import lax

D = 7168
QR = 1536
LAT = 512
NOPE = 128
ROPE = 64
VD = 128
HEADS = 64
SLAB = 128
TOKENS = 4096
NSLAB = 32
N_TP = 16


def draw_kv_latent(key, part):
    key = jax.random.fold_in(key, 11)
    first_key = jax.random.fold_in(key, 0)
    shape = (TOKENS, LAT + ROPE)
    values = jnp.clip(jax.random.normal(first_key, shape, jnp.float32), -6.0, 6.0)
    return values.astype(jnp.bfloat16)


def draw_block_table(key, part):
    key = jax.random.fold_in(key, 5)
    picks = jax.random.randint(key, (NSLAB, NSLAB), 0, 4)
    ones = (picks > 0).astype(jnp.int32)
    index = jnp.arange(NSLAB, dtype=jnp.int32)
    diagonal = index[:, None] == index[None, :]
    return jnp.where(diagonal, 1, ones).astype(jnp.int32)


def spiked(result, rng, source, target, parts, factor):
    owner, partner = [(jnp.arange(result.shape[position]) // (result.shape[position] // parts)).reshape([-1 if axis == position else 1 for axis in range(result.ndim)]) for position in (source, target)]
    chosen = jax.random.permutation(rng, parts)[partner]
    strong = (owner == chosen) | (owner == (partner + parts // 2) % parts)
    return jnp.where(strong, factor * result, result)


def shard_levels(key, extent, cuts, low, high):
    gain, own = 1.0, jax.random.fold_in(key, 6)
    for dim, blocks in cuts:
        steps = jnp.exp(jax.random.uniform(jax.random.fold_in(own, dim), (blocks,), jnp.float32, low / len(cuts), high / len(cuts)))
        gain = gain * jnp.repeat(steps, extent[dim] // blocks).reshape([-1 if axis == dim else 1 for axis in range(len(extent))])
    return gain


def normal_values(own_key, shape, scale, most, shards=(), kind=jnp.bfloat16):
    level = shard_levels(own_key, shape, shards, -0.22, 0.18) if shards else 1.0
    result = jax.random.normal(own_key, shape, jnp.float32) * scale * level
    return jnp.minimum(jnp.maximum(result, -most), most).astype(kind)


def heavy_noise(key, extent, deviation, most, cuts, heavy, kind=jnp.bfloat16):
    array = deviation * jax.random.normal(key, extent, jnp.float32)
    if cuts:
        array = array * shard_levels(key, extent, cuts, -0.22, 0.18)
    return jnp.clip(spiked(array, jax.random.fold_in(key, 3), *heavy), -most, most).astype(kind)


def setup_inputs(seed: int = 0) -> dict:
    streams_of = jax.random.split(jax.random.key(seed), 9)
    return {
        "c_query": normal_values(streams_of[0], (TOKENS, QR), 1.0, 6.0, ((0, 16),)),
        "w_uq": normal_values(streams_of[1], (QR, HEADS * (NOPE + ROPE)), QR ** -0.5, 0.15625, ((1, 16),)),
        "w_uk": normal_values(streams_of[2], (HEADS, NOPE, LAT), NOPE ** -0.5, 0.5, ((0, 16),)),
        "w_uv": normal_values(streams_of[3], (HEADS, LAT, VD), LAT ** -0.5, 0.25, ((0, 16),)),
        "w_out": heavy_noise(streams_of[4], (HEADS * VD, D), (HEADS * VD) ** -0.5, 0.09375, ((0, 16),), (0, 1, 16, 2.0)),
        "kv_latent": draw_kv_latent(jax.random.fold_in(streams_of[8], 71), 0),
        "slab_order": jax.random.permutation(streams_of[6], NSLAB).astype(jnp.int32),
        "block_table": draw_block_table(jax.random.fold_in(streams_of[8], 71), 0),
    }


def rotate_pairs(values, angles_base):
    half = values.shape[-1] // 2
    freqs = 10000.0 ** (-jnp.arange(half, dtype=jnp.float32) / half)
    angles = angles_base[:, None] * freqs[None, :]
    cosine = jnp.cos(angles)[:, None, :]
    sine = jnp.sin(angles)[:, None, :]
    first = values[..., :half]
    second = values[..., half:]
    return jnp.concatenate([first * cosine - second * sine, second * cosine + first * sine], axis=-1)


def reference(c_query, w_uq, w_uk, w_uv, w_out, kv_latent, slab_order, block_table):
    width = NOPE + ROPE
    query = jnp.dot(c_query, w_uq, preferred_element_type=jnp.float32).reshape(TOKENS, HEADS, width)
    q_nope = query[..., :NOPE].astype(jnp.bfloat16)
    q_lat = jnp.einsum("thn,hnl->thl", q_nope.astype(jnp.float32), w_uk.astype(jnp.float32)).astype(jnp.bfloat16)
    rows = jnp.arange(TOKENS, dtype=jnp.int32)
    seq = slab_order[rows // SLAB].astype(jnp.int32)
    pos = (seq * SLAB + rows % SLAB).astype(jnp.int32)
    q_rot = rotate_pairs(query[..., NOPE:], pos.astype(jnp.float32)).astype(jnp.bfloat16)
    keys = kv_latent.astype(jnp.float32)
    latent = keys[:, :LAT]
    rotary = keys[:, LAT:]
    scale = width ** -0.5

    def one_block(index):
        first = (index * SLAB).astype(jnp.int32)
        lat_rows = lax.dynamic_slice_in_dim(q_lat, first, SLAB, 0).astype(jnp.float32)
        rot_rows = lax.dynamic_slice_in_dim(q_rot, first, SLAB, 0).astype(jnp.float32)
        pos_rows = lax.dynamic_slice_in_dim(pos, first, SLAB, 0)
        seq_rows = lax.dynamic_slice_in_dim(seq, first, SLAB, 0)
        score = (jnp.einsum("thl,jl->thj", lat_rows, latent) + jnp.einsum("thr,jr->thj", rot_rows, rotary)) * scale
        allowed = block_table[seq_rows][:, seq] == 1
        visible = allowed & (pos[None, :] <= pos_rows[:, None])
        score = jnp.where(visible[:, None, :], score, -jnp.inf)
        top = jnp.max(score, axis=-1, keepdims=True)
        expo = jnp.exp(score - top)
        denom = jnp.sum(expo, axis=-1)
        probs = expo.astype(jnp.bfloat16).astype(jnp.float32)
        mixed = jnp.einsum("thj,jl->thl", probs, latent) / denom[..., None]
        return mixed.astype(jnp.bfloat16)

    o_lat = lax.map(one_block, jnp.arange(NSLAB, dtype=jnp.int32)).reshape(TOKENS, HEADS, LAT)
    o_head = jnp.einsum("thl,hlv->thv", o_lat.astype(jnp.float32), w_uv.astype(jnp.float32)).astype(jnp.bfloat16)
    group_heads = HEADS // N_TP
    grouped = jnp.transpose(o_head.reshape(TOKENS, N_TP, group_heads * VD), (1, 0, 2))
    weights = w_out.reshape(N_TP, group_heads * VD, D)

    def add_group(total, pair):
        part = jnp.dot(pair[0], pair[1], preferred_element_type=jnp.float32).astype(jnp.bfloat16)
        part = lax.optimization_barrier(part)
        return total + part.astype(jnp.float32), None

    total, unused = lax.scan(add_group, jnp.zeros((TOKENS, D), jnp.float32), (grouped, weights))
    return total.astype(jnp.bfloat16)
```

```python
import jax
import jax.numpy as jnp
import numpy as np
from jax import lax
from jax.experimental import pallas as pl
from jax.experimental.pallas import tpu as pltpu
from jax.sharding import PartitionSpec as P

MESH = pl.DeviceIdType.MESH
SLAB = 128
TOK = 256
HALF = TOK // 2
HEADS = 4
NOPE = 128
ROPE = 64
LAT = 512
KEY = LAT + ROPE
QR = 1536
VD = 128
GROUP = HEADS * VD
FEAT = 448
NZ = 8
SIDE = NZ * FEAT
WINDOW = 512
PAIR = 2 * FEAT
SCALE = float((NOPE + ROPE) ** -0.5 * np.log2(np.e))
FILL = -1e30

OWN_UP, OWN_DOWN, OWN_P = 0, 2, 4
P_UP, P_DOWN, FAR_UP, FAR_DOWN, FAR_P = 6, 8, 10, 11, 12
SIB = 14
N_KV = 22


def dot(a, b):
    return jnp.dot(a, b, preferred_element_type=jnp.float32)


def kernel(
    cq_hbm, wuq_hbm, wuk_hbm, wuv_hbm, wout_hbm, kv_hbm, order_ref, table_ref, freq_ref,
    out_ref,
    cq, wuq, wuk, wuv, wown, woth, kvbuf, qbuf, acc, top, den, oown, ooth, packed, landed,
    load_sem, kv_send, kv_recv, w_send, w_recv, o_send, o_recv, r_send, r_recv,
):
    ctx = lax.axis_index("ctx")
    tp = lax.axis_index("tp")
    core = lax.rem(ctx, 2)
    yh = lax.rem(lax.div(ctx, 2), 2)
    x = lax.div(ctx, 4)
    yl = lax.div(tp, NZ)
    z = lax.rem(tp, NZ)

    def at(dx, flip_h, flip_l, dz, flip_core):
        nx = lax.rem(x + dx + 4, 4)
        nh = 1 - yh if flip_h else yh
        nl = 1 - yl if flip_l else yl
        nz = lax.rem(z + dz + NZ, NZ)
        nc = 1 - core if flip_core else core
        return ((nx * 2 + nh) * 2 + nc, nl * NZ + nz)

    up_x, down_x = at(1, 0, 0, 0, 0), at(-1, 0, 0, 0, 0)
    across, beside = at(0, 1, 1, 0, 0), at(0, 0, 1, 0, 0)
    up_z, down_z = at(0, 0, 0, 1, 0), at(0, 0, 0, -1, 0)
    sibling = at(0, 0, 0, 0, 1)

    def block(dx, flip_h, flip_core):
        return at(dx, flip_h, 0, 0, flip_core)[0]

    loads = [
        pltpu.make_async_copy(cq_hbm, cq, load_sem.at[0]),
        pltpu.make_async_copy(wuq_hbm, wuq, load_sem.at[1]),
        pltpu.make_async_copy(wuk_hbm, wuk, load_sem.at[2]),
        pltpu.make_async_copy(kv_hbm, kvbuf.at[ctx], load_sem.at[3]),
        pltpu.make_async_copy(wuv_hbm, wuv, load_sem.at[4]),
        pltpu.make_async_copy(
            wout_hbm.at[:, pl.ds(pl.multiple_of(yl * SIDE, 128), SIDE)], wown, load_sem.at[5]
        ),
    ]
    for load in loads:
        load.start()

    barrier = pltpu.get_barrier_semaphore()
    for device in (up_x, down_x, across, beside, up_z, down_z, sibling):
        pl.semaphore_signal(barrier, inc=1, device_id=device, device_id_type=MESH)
    pl.semaphore_wait(barrier, 7)

    def rows(h):
        return pl.ds(h * HALF, HALF)

    def kv_copy(index, b, h, device, own=False):
        return pltpu.make_async_remote_copy(
            src_ref=kv_hbm.at[rows(h)] if own else kvbuf.at[b, rows(h)],
            dst_ref=kvbuf.at[b, rows(h)],
            send_sem=kv_send.at[index],
            recv_sem=kv_recv.at[index],
            device_id=device,
            device_id_type=MESH,
        )

    def sib_copy(k, b, own=False):
        return pltpu.make_async_remote_copy(
            src_ref=kv_hbm if own else kvbuf.at[b],
            dst_ref=kvbuf.at[b],
            send_sem=kv_send.at[SIB + k],
            recv_sem=kv_recv.at[SIB + k],
            device_id=sibling,
            device_id_type=MESH,
        )

    places = ((0, 0), (-1, 0), (1, 0), (0, 1), (2, 0), (-1, 1), (1, 1), (2, 1))
    blocks = [block(dx, flip, 0) for dx, flip in places]
    sib_blocks = [block(dx, flip, 1) for dx, flip in places]
    own, low, high, cross, far, low_cross, high_cross, far_cross = blocks

    own_sends = []
    for h in range(2):
        own_sends += [
            kv_copy(OWN_UP + h, own, h, up_x, True),
            kv_copy(OWN_P + h, own, h, across, True),
            kv_copy(OWN_DOWN + h, own, h, down_x, True),
        ]
    own_sends.insert(0, sib_copy(0, own, True))
    for copy in own_sends:
        copy.start()

    def group_columns(g):
        base = lax.div(z, 2)
        steps = (0, 2 * lax.rem(z, 2) - 1, 1 - 2 * lax.rem(z, 2), 2)
        return lax.rem(base + steps[g] + 4, 4) * PAIR

    def quarter(dx, dc):
        return lax.rem(x + dx + 4, 4) * 128 + (1 - core if dc else core) * 64

    def w_copy(index, src, src_base, r, g, device):
        cols = group_columns(g)
        return pltpu.make_async_remote_copy(
            src_ref=src.at[pl.ds(r, 64), pl.ds(pl.multiple_of(src_base + cols, 128), PAIR)],
            dst_ref=woth.at[pl.ds(r, 64), pl.ds(pl.multiple_of(cols, 128), PAIR)],
            send_sem=w_send.at[index, g],
            recv_sem=w_recv.at[index, g],
            device_id=device,
            device_id_type=MESH,
        )

    other = (1 - yl) * SIDE
    w_dx = (0, 2, -1, 1)

    def w_beside(g):
        return w_copy(0, wout_hbm, other, quarter(0, 0), g, beside)

    def w_across(g):
        return w_copy(1, wout_hbm, other, quarter(2, 0), g, across)

    def w_up(g):
        return w_copy(2, woth, 0, quarter(0, 0), g, up_x)

    def w_down(g):
        return w_copy(3, woth, 0, quarter(0, 0), g, down_x)

    def w_landed(i, g):
        return w_copy(i, woth, 0, quarter(w_dx[i % 4], i // 4), g, sibling)

    def w_sib(i, g):
        return w_copy(4 + i, woth, 0, quarter(w_dx[i], 0), g, sibling)

    for g in range(4):
        w_beside(g).start()

    lane = lax.broadcasted_iota(jnp.int32, (SLAB, 128), 1)
    row = lax.broadcasted_iota(jnp.int32, (SLAB, 128), 0)
    delta = lane - row
    seqs = [order_ref[2 * ctx + a] for a in range(2)]
    loads[0].wait()
    loads[1].wait()
    loads[2].wait()
    first_half = lax.rem(lane, 64) < 32
    for a in range(2):
        pos = (seqs[a] * SLAB + row).astype(jnp.float32)
        angle = pos * freq_ref[0:1, :]
        cosine = jnp.cos(angle) * SCALE
        sine = jnp.sin(angle) * SCALE
        sine = jnp.where(first_half, -sine, sine)
        rows_a = pl.ds(a * SLAB, SLAB)
        for k in range(2):
            q = dot(cq[rows_a, :], wuq[:, k * 384 : (k + 1) * 384])
            shifted = pltpu.roll(q, 64, 1)
            nopes = (q[:, 0:128], shifted[:, 256:384])
            pair = jnp.where(lane < 64, q[:, 128:256], q[:, 256:384])
            swapped = jnp.where(first_half, pltpu.roll(pair, 96, 1), pltpu.roll(pair, 32, 1))
            turned = pair * cosine + swapped * sine
            ropes = (turned, pltpu.roll(turned, 64, 1))
            for j in range(2):
                h = 2 * k + j
                rows_h = pl.ds(h * SLAB, SLAB)
                q_lat = dot(nopes[j].astype(jnp.bfloat16), wuk[h]) * SCALE
                qbuf[a, rows_h, 0:LAT] = q_lat.astype(jnp.bfloat16)
                qbuf[a, rows_h, LAT:KEY] = ropes[j][:, 0:ROPE].astype(jnp.bfloat16)

    top[...] = jnp.full_like(top, FILL)
    den[...] = jnp.zeros_like(den)
    acc[...] = jnp.zeros_like(acc)

    def attend(pair):
        keys = kvbuf[pl.ds(2 * pair, 2)].reshape(2 * TOK, KEY)
        values = keys[:, 0:LAT]
        for a in range(2):
            bias = []
            for k in range(4):
                seq_k = order_ref[4 * pair + k]
                allowed = table_ref[seqs[a], seq_k] == 1
                limit = jnp.where(seq_k < seqs[a], SLAB, jnp.where(seq_k == seqs[a], 0, -SLAB))
                limit = jnp.where(allowed, limit, -SLAB)
                bias.append(jnp.where(delta <= limit, 0.0, FILL))
            bias = jnp.concatenate(bias, axis=1)
            score = lax.dot_general(
                qbuf[a], keys, (((1,), (1,)), ((), ())), preferred_element_type=jnp.float32
            )
            score = (score.reshape(HEADS, SLAB, 2 * TOK) + bias[None]).reshape(HEADS * SLAB, 2 * TOK)
            old = top[a]
            new = jnp.maximum(old, jnp.max(score, axis=1, keepdims=True))
            top[a] = new
            shrink = jnp.exp2(old - new)
            weight = jnp.exp2(score - new[:, 0:1])
            part = weight[:, 0:128]
            for k in range(1, 4):
                part = part + weight[:, k * 128 : (k + 1) * 128]
            den[a] = den[a] * shrink + part
            acc[a] = acc[a] * shrink[:, 0:1] + dot(weight.astype(jnp.bfloat16), values)

    def finish(a):
        total = jnp.sum(den[a], axis=1, keepdims=True)
        o_lat = (acc[a] / total).astype(jnp.bfloat16)
        for h in range(HEADS):
            o_head = dot(o_lat[h * SLAB : (h + 1) * SLAB], wuv[h])
            oown[pl.ds(a * SLAB, SLAB), h * VD : (h + 1) * VD] = o_head.astype(jnp.bfloat16)

    def o_copy(k):
        part = pl.ds(k * 64, 64)
        return pltpu.make_async_remote_copy(
            src_ref=oown.at[part],
            dst_ref=ooth.at[part],
            send_sem=o_send.at[k],
            recv_sem=o_recv.at[k],
            device_id=beside,
            device_id_type=MESH,
        )

    def step(i, carry):
        @pl.when(i == 0)
        def _():
            loads[3].wait()
            sib_copy(0, sib_blocks[0], True).wait_recv()

        @pl.when(i == 1)
        def _():
            kv_copy(OWN_UP, low, 0, up_x).wait_recv()
            kv_copy(FAR_UP, low, 0, up_x).start()
            kv_copy(OWN_P, cross, 0, across).wait_recv()
            kv_copy(P_UP, cross, 0, up_x).start()
            kv_copy(P_DOWN, cross, 0, down_x).start()
            kv_copy(OWN_DOWN, high, 0, down_x).wait_recv()
            kv_copy(OWN_DOWN + 1, high, 1, down_x).wait_recv()
            kv_copy(FAR_DOWN, high, 1, down_x).start()
            kv_copy(OWN_P + 1, cross, 1, across).wait_recv()
            kv_copy(P_UP + 1, cross, 1, up_x).start()
            kv_copy(P_DOWN + 1, cross, 1, down_x).start()
            kv_copy(OWN_UP + 1, low, 1, up_x).wait_recv()
            for k in range(1, 4):
                sib_copy(k, blocks[k]).start()
            sib_copy(1, sib_blocks[1]).wait_recv()

        @pl.when(i == 2)
        def _():
            kv_copy(FAR_UP, far, 0, up_x).wait_recv()
            kv_copy(FAR_P, far, 0, across).start()
            kv_copy(FAR_DOWN, far, 1, down_x).wait_recv()
            kv_copy(FAR_P + 1, far, 1, across).start()
            sib_copy(4, far).start()
            sib_copy(2, sib_blocks[2]).wait_recv()
            for g in range(4):
                w_across(g).start()

        @pl.when(i == 3)
        def _():
            sib_copy(3, sib_blocks[3]).wait_recv()

        @pl.when(i == 4)
        def _():
            sib_copy(4, sib_blocks[4]).wait_recv()

        @pl.when(i == 5)
        def _():
            for h in range(2):
                kv_copy(P_UP + h, low_cross, h, up_x).wait_recv()
                kv_copy(P_DOWN + h, high_cross, h, down_x).wait_recv()
            for k in range(5, 7):
                sib_copy(k, blocks[k]).start()
            for g in range(4):
                w_landed(0, g).wait_recv()
                w_up(g).start()
                w_down(g).start()
                w_sib(0, g).start()
            sib_copy(5, sib_blocks[5]).wait_recv()

        @pl.when(i == 6)
        def _():
            for h in range(2):
                kv_copy(FAR_P + h, far_cross, h, across).wait_recv()
            sib_copy(7, far_cross).start()
            sib_copy(6, sib_blocks[6]).wait_recv()

        @pl.when(i == 7)
        def _():
            sib_copy(7, sib_blocks[7]).wait_recv()

        pair = lax.div(own, 2)
        for k in range(1, 8):
            pair = jnp.where(i == k, lax.div(blocks[k], 2), pair)
        attend(pair)
        return carry

    lax.fori_loop(0, 8, step, 0)
    loads[4].wait()
    for a in range(2):
        finish(a)
        for u in range(2):
            o_copy(2 * a + u).start()
    loads[5].wait()

    lane32 = lax.broadcasted_iota(jnp.int32, (32, 128), 1)

    def r_copy(way, s, u):
        return pltpu.make_async_remote_copy(
            src_ref=packed.at[way, s, u],
            dst_ref=landed.at[way, s, u],
            send_sem=r_send.at[way, s, u],
            recv_sem=r_recv.at[way, s, u],
            device_id=(up_z, down_z)[way],
            device_id_type=MESH,
        )

    def reduce_step(s, carry):
        for g in range(4):

            @pl.when(s == (0, 0, 1, 2)[g])
            def _():
                w_landed(1, g).wait_recv()
                w_sib(1, g).start()
                for i in (2, 3):
                    w_landed(i, g).wait_recv()
                    w_sib(i, g).start()
                for i in range(4, 8):
                    w_landed(i, g).wait_recv()

        for way in range(2):
            d = lax.rem(z + (NZ - 1 - s if way == 0 else 1 + s) + NZ, NZ)
            odd = lax.rem(d, 2)
            even = odd == 0
            start = pl.multiple_of(d * FEAT - odd * 64, 128)
            window = pl.ds(start, WINDOW)
            rows_w = pl.ds(way * SLAB, SLAB)

            @pl.when(s == 0)
            def _():
                for u in range(2):
                    o_copy(2 * way + u).wait_recv()

            part = dot(oown[rows_w, :], wown[:, window]) + dot(ooth[rows_w, :], woth[:, window])
            main = jnp.where(even, part[:, 0:384], part[:, 128:512])
            tail = jnp.where(even, part[:, 384:512], part[:, 0:128])
            for u in range(2):
                t = u * 64
                first, second = tail[t : t + 32], tail[t + 32 : t + 64]
                tails = jnp.where(
                    even,
                    jnp.where(lane32 < 64, first, pltpu.roll(second, 64, 1)),
                    jnp.where(lane32 < 64, pltpu.roll(first, 64, 1), second),
                )
                total = jnp.concatenate([main[t : t + 32], main[t + 32 : t + 64], tails], axis=1)

                @pl.when(s == 0)
                def _():
                    packed[way, 0, u] = total.astype(jnp.bfloat16)

                @pl.when(s > 0)
                def _():
                    before = jnp.maximum(s - 1, 0)
                    r_copy(way, before, u).wait_recv()
                    packed[way, s, u] = (total + landed[way, before, u].astype(jnp.float32)).astype(
                        jnp.bfloat16
                    )

                @pl.when(s < NZ - 1)
                def _():
                    r_copy(way, jnp.minimum(s, NZ - 2), u).start()

        return carry

    lax.fori_loop(0, NZ, reduce_step, 0)

    even = lax.rem(z, 2) == 0
    for way in range(2):
        for u in range(2):
            whole = packed[way, NZ - 1, u].astype(jnp.float32)
            tails = whole[:, 768:896]
            turned = pltpu.roll(tails, 64, 1)
            for k in range(2):
                main = whole[:, k * 384 : (k + 1) * 384]
                lower, upper = (tails, turned) if k == 0 else (turned, tails)
                plain = jnp.concatenate([main, lower], axis=1)
                moved = pltpu.roll(jnp.concatenate([upper if k else turned, main], axis=1), 448, 1)
                result = jnp.where(even, plain, moved)[:, 0:FEAT]
                out_ref[pl.ds(way * SLAB + u * 64 + k * 32, 32), :] = result.astype(jnp.bfloat16)

    for copy in own_sends:
        copy.wait_send()
    for h in range(2):
        kv_copy(P_UP + h, cross, h, up_x).wait_send()
        kv_copy(P_DOWN + h, cross, h, down_x).wait_send()
        kv_copy(FAR_P + h, far, h, across).wait_send()
    kv_copy(FAR_UP, low, 0, up_x).wait_send()
    kv_copy(FAR_DOWN, high, 1, down_x).wait_send()
    for k in range(1, 8):
        sib_copy(k, blocks[k]).wait_send()
    for g in range(4):
        for copy in (w_beside(g), w_across(g), w_up(g), w_down(g)):
            copy.wait_send()
        for i in range(4):
            w_sib(i, g).wait_send()
    for k in range(4):
        o_copy(k).wait_send()
    for way in range(2):
        for s in range(NZ - 1):
            for u in range(2):
                r_copy(way, s, u).wait_send()


def shards(c_query, w_uq, w_uk, w_uv, w_out, kv_latent, slab_order, block_table):
    freqs = 10000.0 ** (-jnp.arange(ROPE // 2, dtype=jnp.float32) / (ROPE // 2))
    freqs = jnp.broadcast_to(jnp.tile(freqs, 4)[None, :], (8, 128))
    bf16 = jnp.bfloat16
    dma = pltpu.SemaphoreType.DMA
    return pl.pallas_call(
        kernel,
        out_shape=jax.ShapeDtypeStruct((TOK, FEAT), bf16),
        in_specs=[pl.BlockSpec(memory_space=pl.ANY)] * 6
        + [pl.BlockSpec(memory_space=pltpu.SMEM)] * 2
        + [pl.BlockSpec(memory_space=pltpu.VMEM)],
        out_specs=pl.BlockSpec(memory_space=pltpu.VMEM),
        scratch_shapes=[
            pltpu.VMEM((TOK, QR), bf16),
            pltpu.VMEM((QR, HEADS * (NOPE + ROPE)), bf16),
            pltpu.VMEM((HEADS, NOPE, LAT), bf16),
            pltpu.VMEM((HEADS, LAT, VD), bf16),
            pltpu.VMEM((GROUP, SIDE), bf16),
            pltpu.VMEM((GROUP, SIDE), bf16),
            pltpu.VMEM((16, TOK, KEY), bf16),
            pltpu.VMEM((2, HEADS * SLAB, KEY), bf16),
            pltpu.VMEM((2, HEADS * SLAB, LAT), jnp.float32),
            pltpu.VMEM((2, HEADS * SLAB, 128), jnp.float32),
            pltpu.VMEM((2, HEADS * SLAB, 128), jnp.float32),
            pltpu.VMEM((TOK, GROUP), bf16),
            pltpu.VMEM((TOK, GROUP), bf16),
            pltpu.VMEM((2, NZ, 2, 32, PAIR), bf16),
            pltpu.VMEM((2, NZ - 1, 2, 32, PAIR), bf16),
            dma((6,)),
            dma((N_KV,)),
            dma((N_KV,)),
            dma((8, 4)),
            dma((8, 4)),
            dma((4,)),
            dma((4,)),
            dma((2, NZ - 1, 2)),
            dma((2, NZ - 1, 2)),
        ],
        compiler_params=pltpu.CompilerParams(
            collective_id=0, has_side_effects=True, vmem_limit_bytes=58 * 2**20
        ),
        name="attention",
    )(c_query, w_uq, w_uk, w_uv, w_out, kv_latent, slab_order, block_table, freqs)


def solution(mesh):
    in_specs = (
        P("ctx", None),
        P(None, "tp"),
        P("tp", None, None),
        P("tp", None, None),
        P("tp", None),
        P("ctx", None),
        P(),
        P(),
    )
    return jax.shard_map(
        shards, mesh=mesh, in_specs=in_specs, out_specs=P("ctx", "tp"), check_vma=False
    )
```

```python
import jax
import jax.numpy as jnp
import numpy as np
from jax import lax
from jax.experimental import pallas as pl
from jax.experimental.pallas import tpu as pltpu
from jax.sharding import PartitionSpec as P

MESH = pl.DeviceIdType.MESH
SLAB = 128
TOK = 256
HALF = TOK // 2
HEADS = 4
NOPE = 128
ROPE = 64
LAT = 512
KEY = LAT + ROPE
QR = 1536
VD = 128
GROUP = HEADS * VD
FEAT = 448
NZ = 8
SIDE = NZ * FEAT
WINDOW = 512
PAIR = 2 * FEAT
SCALE = float((NOPE + ROPE) ** -0.5 * np.log2(np.e))
FILL = -1e30

OWN_UP, OWN_DOWN, OWN_P = 0, 2, 4
P_UP, P_DOWN, FAR_UP, FAR_DOWN, FAR_P = 6, 8, 10, 12, 14
SIB = 16
N_KV = 32


def dot(a, b):
    return jnp.dot(a, b, preferred_element_type=jnp.float32)


def kernel(
    cq_hbm, wuq_hbm, wuk_hbm, wuv_hbm, wout_hbm, kv_hbm, order_ref, table_ref,
    out_ref,
    cq, wuq, wuk, wuv, wown, woth, kvbuf, qbuf, acc, top, den, oown, ooth, packed, landed, final, parts,
    load_sem, kv_send, kv_recv, w_send, w_recv, o_send, o_recv, r_send, r_recv,
):
    ctx = lax.axis_index("ctx")
    tp = lax.axis_index("tp")
    core = lax.rem(ctx, 2)
    yh = lax.rem(lax.div(ctx, 2), 2)
    x = lax.div(ctx, 4)
    yl = lax.div(tp, NZ)
    z = lax.rem(tp, NZ)

    def at(dx, flip_h, flip_l, dz, flip_core):
        nx = lax.rem(x + dx + 4, 4)
        nh = 1 - yh if flip_h else yh
        nl = 1 - yl if flip_l else yl
        nz = lax.rem(z + dz + NZ, NZ)
        nc = 1 - core if flip_core else core
        return ((nx * 2 + nh) * 2 + nc, nl * NZ + nz)

    up_x, down_x = at(1, 0, 0, 0, 0), at(-1, 0, 0, 0, 0)
    across, beside = at(0, 1, 1, 0, 0), at(0, 0, 1, 0, 0)
    up_z, down_z = at(0, 0, 0, 1, 0), at(0, 0, 0, -1, 0)
    sibling = at(0, 0, 0, 0, 1)

    def block(dx, flip_h, flip_core):
        return at(dx, flip_h, 0, 0, flip_core)[0]

    loads = [
        pltpu.make_async_copy(cq_hbm, cq, load_sem.at[0]),
        pltpu.make_async_copy(wuq_hbm, wuq, load_sem.at[1]),
        pltpu.make_async_copy(wuk_hbm, wuk, load_sem.at[2]),
        pltpu.make_async_copy(kv_hbm.at[:, 0:SLAB], kvbuf.at[2 * ctx], load_sem.at[3]),
        pltpu.make_async_copy(wuv_hbm, wuv, load_sem.at[4]),
        pltpu.make_async_copy(
            wout_hbm.at[:, pl.ds(pl.multiple_of(yl * SIDE, 128), SIDE)], wown, load_sem.at[5]
        ),
        pltpu.make_async_copy(kv_hbm.at[:, SLAB:TOK], kvbuf.at[2 * ctx + 1], load_sem.at[6]),
    ]
    for load in loads:
        load.start()

    barrier = pltpu.get_barrier_semaphore()
    for device in (up_x, down_x, across, beside, up_z, down_z, sibling):
        pl.semaphore_signal(barrier, inc=1, device_id=device, device_id_type=MESH)
    pl.semaphore_wait(barrier, 7)

    def source(b, h, own):
        return kv_hbm.at[:, h * SLAB : (h + 1) * SLAB] if own else kvbuf.at[2 * b + h]

    def kv_copy(index, b, h, device, own=False):
        return pltpu.make_async_remote_copy(
            src_ref=source(b, h, own),
            dst_ref=kvbuf.at[2 * b + h],
            send_sem=kv_send.at[index + h],
            recv_sem=kv_recv.at[index + h],
            device_id=device,
            device_id_type=MESH,
        )

    def part_copy(index, b, h, part, device):
        rows = pl.ds(part * (KEY // 2), KEY // 2)
        return pltpu.make_async_remote_copy(
            src_ref=kvbuf.at[2 * b + h, rows],
            dst_ref=kvbuf.at[2 * b + h, rows],
            send_sem=kv_send.at[index + h],
            recv_sem=kv_recv.at[index + h],
            device_id=device,
            device_id_type=MESH,
        )

    def sib_copy(k, b, h, own=False):
        return kv_copy(SIB + 2 * k, b, h, sibling, own)

    places = ((0, 0), (-1, 0), (1, 0), (0, 1), (2, 0), (-1, 1), (1, 1), (2, 1))
    blocks = [block(dx, flip, 0) for dx, flip in places]
    sib_blocks = [block(dx, flip, 1) for dx, flip in places]
    own, low, high, cross, far, low_cross, high_cross, far_cross = blocks

    own_sends = []
    for h in range(2):
        own_sends += [
            kv_copy(OWN_UP, own, h, up_x, True),
            kv_copy(OWN_DOWN, own, h, down_x, True),
            kv_copy(OWN_P, own, h, across, True),
            sib_copy(0, own, h, True),
        ]
    for copy in own_sends:
        copy.start()

    def group_columns(g):
        base = lax.div(z, 2)
        steps = (2, 1 - 2 * lax.rem(z, 2), 2 * lax.rem(z, 2) - 1, 0)
        return lax.rem(base + steps[g] + 4, 4) * PAIR

    def quarter(dx, dc):
        return lax.rem(x + dx + 4, 4) * 128 + (1 - core if dc else core) * 64

    def w_copy(index, src, src_base, r, g, device):
        cols = group_columns(g)
        return pltpu.make_async_remote_copy(
            src_ref=src.at[pl.ds(r, 64), pl.ds(pl.multiple_of(src_base + cols, 128), PAIR)],
            dst_ref=woth.at[pl.ds(r, 64), pl.ds(pl.multiple_of(cols, 128), PAIR)],
            send_sem=w_send.at[index, g],
            recv_sem=w_recv.at[index, g],
            device_id=device,
            device_id_type=MESH,
        )

    other = (1 - yl) * SIDE
    w_dx = (0, 2, -1, 1)

    def w_beside(g):
        return w_copy(0, wout_hbm, other, quarter(0, 0), g, beside)

    def w_across(g):
        return w_copy(1, wout_hbm, other, quarter(2, 0), g, across)

    def w_up(g):
        return w_copy(2, woth, 0, quarter(0, 0), g, up_x)

    def w_down(g):
        return w_copy(3, woth, 0, quarter(0, 0), g, down_x)

    def w_landed(i, g):
        return w_copy(i, woth, 0, quarter(w_dx[i % 4], i // 4), g, sibling)

    def w_sib(i, g):
        return w_copy(4 + i, woth, 0, quarter(w_dx[i], 0), g, sibling)

    for g in range(4):
        w_beside(g).start()

    lane = lax.broadcasted_iota(jnp.int32, (SLAB, 128), 1)
    row = lax.broadcasted_iota(jnp.int32, (SLAB, 128), 0)
    delta = lane - row
    seqs = [order_ref[2 * ctx + a] for a in range(2)]
    loads[0].wait()
    loads[1].wait()
    loads[2].wait()
    first_half = lax.rem(lane, 64) < 32
    freq = jnp.exp(lax.rem(lane, 32).astype(jnp.float32) * float(-np.log(10000.0) / 32))
    for a in range(2):
        pos = (seqs[a] * SLAB + row).astype(jnp.float32)
        angle = pos * freq
        cosine = jnp.cos(angle) * SCALE
        sine = jnp.sin(angle) * SCALE
        sine = jnp.where(first_half, -sine, sine)
        rows_a = pl.ds(a * SLAB, SLAB)
        for k in range(2):
            q = dot(cq[rows_a, :], wuq[:, k * 384 : (k + 1) * 384])
            shifted = pltpu.roll(q, 64, 1)
            nopes = (q[:, 0:128], shifted[:, 256:384])
            pair = jnp.where(lane < 64, q[:, 128:256], q[:, 256:384])
            swapped = jnp.where(first_half, pltpu.roll(pair, 96, 1), pltpu.roll(pair, 32, 1))
            turned = pair * cosine + swapped * sine
            ropes = (turned, pltpu.roll(turned, 64, 1))
            for j in range(2):
                h = 2 * k + j
                rows_h = pl.ds(h * SLAB, SLAB)
                q_lat = dot(nopes[j].astype(jnp.bfloat16), wuk[h]) * SCALE
                qbuf[a, rows_h, 0:LAT] = q_lat.astype(jnp.bfloat16)
                qbuf[a, rows_h, LAT:KEY] = ropes[j][:, 0:ROPE].astype(jnp.bfloat16)

    top[...] = jnp.full_like(top, FILL)
    den[...] = jnp.zeros_like(den)
    acc[...] = jnp.zeros_like(acc)

    def attend(slabs):
        keys = jnp.concatenate([kvbuf[slab] for slab in slabs], axis=1)
        width = len(slabs) * SLAB
        found = [order_ref[slab] for slab in slabs]

        def scores(a):
            return dot(qbuf[a], keys)

        def absorb(a, score):
            bias = []
            for seq_k in found:
                allowed = table_ref[seqs[a], seq_k] == 1
                limit = jnp.where(seq_k < seqs[a], SLAB, jnp.where(seq_k == seqs[a], 0, -SLAB))
                limit = jnp.where(allowed, limit, -SLAB)
                bias.append(jnp.where(delta <= limit, 0.0, FILL))
            bias = jnp.concatenate(bias, axis=1)
            score = (score.reshape(HEADS, SLAB, width) + bias[None]).reshape(HEADS * SLAB, width)
            old = top[a]
            new = jnp.maximum(old, jnp.max(score, axis=1, keepdims=True))
            top[a] = new
            shrink = jnp.exp2(old - new)
            weight = jnp.exp2(score - new[:, 0:1])
            part = weight[:, 0:128]
            for k in range(1, len(slabs)):
                part = part + weight[:, k * 128 : (k + 1) * 128]
            den[a] = den[a] * shrink + part
            mixed = lax.dot_general(
                weight.astype(jnp.bfloat16),
                keys[0:LAT],
                (((1,), (1,)), ((), ())),
                preferred_element_type=jnp.float32,
            )
            acc[a] = acc[a] * shrink[:, 0:1] + mixed

        first, second = scores(0), scores(1)
        absorb(0, first)
        absorb(1, second)

    def finish(a):
        total = jnp.sum(den[a], axis=1, keepdims=True)
        o_lat = (acc[a] / total).astype(jnp.bfloat16)
        for h in range(HEADS):
            o_head = dot(o_lat[h * SLAB : (h + 1) * SLAB], wuv[h])
            oown[pl.ds(a * SLAB, SLAB), h * VD : (h + 1) * VD] = o_head.astype(jnp.bfloat16)

    def o_copy(a):
        part = pl.ds(a * SLAB, SLAB)
        return pltpu.make_async_remote_copy(
            src_ref=oown.at[part],
            dst_ref=ooth.at[part],
            send_sem=o_send.at[a],
            recv_sem=o_recv.at[a],
            device_id=beside,
            device_id_type=MESH,
        )

    def land(pairs):
        for k, h in pairs:
            sib_copy(k, sib_blocks[k], h).wait_recv()

    def step(i, carry):
        @pl.when(i == 0)
        def _():
            loads[3].wait()
            loads[6].wait()
            land([(0, 0), (0, 1)])

        @pl.when(i == 1)
        def _():
            kv_copy(OWN_UP, low, 0, up_x).wait_recv()
            part_copy(FAR_UP, low, 0, 0, up_x).start()
            kv_copy(OWN_DOWN, high, 0, down_x).wait_recv()
            part_copy(FAR_DOWN, high, 0, 1, down_x).start()
            sib_copy(1, low, 0).start()
            sib_copy(2, high, 0).start()
            kv_copy(OWN_P, cross, 0, across).wait_recv()
            sib_copy(3, cross, 0).start()
            land([(1, 0), (2, 0), (3, 0)])

        @pl.when(i == 2)
        def _():
            kv_copy(OWN_UP, low, 1, up_x).wait_recv()
            part_copy(FAR_UP, low, 1, 0, up_x).start()
            kv_copy(OWN_DOWN, high, 1, down_x).wait_recv()
            part_copy(FAR_DOWN, high, 1, 1, down_x).start()
            kv_copy(P_UP, cross, 0, up_x).start()
            kv_copy(P_DOWN, cross, 0, down_x).start()
            sib_copy(1, low, 1).start()
            sib_copy(2, high, 1).start()
            kv_copy(OWN_P, cross, 1, across).wait_recv()
            kv_copy(P_UP, cross, 1, up_x).start()
            kv_copy(P_DOWN, cross, 1, down_x).start()
            sib_copy(3, cross, 1).start()
            land([(1, 1), (2, 1), (3, 1)])

        @pl.when(i == 3)
        def _():
            for h in range(2):
                part_copy(FAR_UP, far, h, 0, up_x).wait_recv()
                part_copy(FAR_DOWN, far, h, 1, down_x).wait_recv()
                kv_copy(FAR_P, far, h, across).start()
                sib_copy(4, far, h).start()
            for g in range(4):
                w_across(g).start()
            land([(4, 0), (4, 1)])

        @pl.when(i == 4)
        def _():
            kv_copy(P_UP, low_cross, 0, up_x).wait_recv()
            sib_copy(5, low_cross, 0).start()
            kv_copy(P_DOWN, high_cross, 0, down_x).wait_recv()
            sib_copy(6, high_cross, 0).start()
            for g in range(4):
                w_landed(0, g).wait_recv()
                w_up(g).start()
                w_down(g).start()
            land([(5, 0), (6, 0)])

        @pl.when(i == 5)
        def _():
            kv_copy(FAR_P, far_cross, 0, across).wait_recv()
            sib_copy(7, far_cross, 0).start()
            kv_copy(P_UP, low_cross, 1, up_x).wait_recv()
            sib_copy(5, low_cross, 1).start()
            kv_copy(P_DOWN, high_cross, 1, down_x).wait_recv()
            sib_copy(6, high_cross, 1).start()
            kv_copy(FAR_P, far_cross, 1, across).wait_recv()
            sib_copy(7, far_cross, 1).start()
            for g in range(4):
                w_sib(0, g).start()
            land([(5, 1), (6, 1), (7, 0), (7, 1)])

        def slabs(k, h):
            return [2 * blocks[k] + h, 2 * sib_blocks[k] + h]

        def pick(choices, at_steps):
            chosen = choices[0]
            for choice, at_step in zip(choices[1:], at_steps):
                chosen = [jnp.where(i == at_step, b, a) for a, b in zip(chosen, choice)]
            return chosen

        @pl.when((i == 0) | (i == 3) | (i == 4))
        def _():
            attend(
                pick(
                    [
                        slabs(0, 0) + slabs(0, 1),
                        slabs(4, 0) + slabs(4, 1),
                        slabs(5, 0) + slabs(6, 0),
                    ],
                    (3, 4),
                )
            )

        @pl.when((i == 1) | (i == 2))
        def _():
            attend(
                pick([slabs(1, 0) + slabs(2, 0) + slabs(3, 0), slabs(1, 1) + slabs(2, 1) + slabs(3, 1)], (2,))
            )

        @pl.when(i == 5)
        def _():
            attend(slabs(5, 1) + slabs(6, 1) + slabs(7, 0) + slabs(7, 1))

        return carry

    lax.fori_loop(0, 6, step, 0)
    loads[4].wait()
    for a in range(2):
        finish(a)
        o_copy(a).start()
    loads[5].wait()

    lane64 = lax.broadcasted_iota(jnp.int32, (64, 128), 1)
    FOUR_UP, FOUR_DOWN, THREE_UP, THREE_DOWN = 0, 4, 8, 11

    def r_copy(k, device):
        return pltpu.make_async_remote_copy(
            src_ref=packed.at[k],
            dst_ref=landed.at[k],
            send_sem=r_send.at[k],
            recv_sem=r_recv.at[k],
            device_id=device,
            device_id_type=MESH,
        )

    def chunk(dz):
        d = lax.rem(z + dz + NZ, NZ)
        odd = lax.rem(d, 2)
        return odd == 0, pl.ds(pl.multiple_of(d * FEAT - odd * 64, 128), WINDOW)

    def mine(dz):
        parts[dz % NZ] = dot(oown[...], wown[:, chunk(dz)[1]])

    def others(dz, a=None):
        rows_a = pl.ds(0, TOK) if a is None else pl.ds(a * SLAB, SLAB)
        parts[dz % NZ, rows_a] += dot(ooth[rows_a, :], woth[:, chunk(dz)[1]])

    def pack(dz, a):
        even = chunk(dz)[0]
        part = parts[dz % NZ, pl.ds(a * SLAB, SLAB)]
        main = jnp.where(even, part[:, 0:384], part[:, 128:512])
        tail = jnp.where(even, part[:, 384:512], part[:, 0:128])
        first, second = tail[0:64], tail[64:128]
        tails = jnp.where(
            even,
            jnp.where(lane64 < 64, first, pltpu.roll(second, 64, 1)),
            jnp.where(lane64 < 64, pltpu.roll(first, 64, 1), second),
        )
        return jnp.concatenate([main[0:64], main[64:128], tails], axis=1)

    def send(k, dz, a, device, follows):
        total = pack(dz, a)
        if follows:
            r_copy(k - 1, device).wait_recv()
            total = total + landed[k - 1].astype(jnp.float32)
        packed[k] = total.astype(jnp.bfloat16)
        r_copy(k, device).start()

    def land_group(g):
        w_landed(1, g).wait_recv()
        w_sib(1, g).start()
        for i in (2, 3):
            w_landed(i, g).wait_recv()
            w_sib(i, g).start()
        for i in range(4, 8):
            w_landed(i, g).wait_recv()

    for dz in (4, 3, -3):
        mine(dz)
    land_group(0)
    o_copy(0).wait_recv()
    others(4, 0)
    send(FOUR_UP, 4, 0, up_z, False)
    o_copy(1).wait_recv()
    others(4, 1)
    send(FOUR_DOWN, 4, 1, down_z, False)
    land_group(1)
    for dz in (3, -3):
        others(dz)
    send(THREE_UP, 3, 1, up_z, False)
    send(THREE_DOWN, -3, 0, down_z, False)
    for t in range(1, 4):
        dz = 4 - t
        send(FOUR_UP + t, dz, 0, up_z, True)
        send(FOUR_DOWN + t, -dz, 1, down_z, True)
        if t < 3:
            land_group(t + 1)
            for nearer in (dz - 1, 1 - dz):
                mine(nearer)
                others(nearer)
            send(THREE_UP + t, dz - 1, 1, up_z, True)
            send(THREE_DOWN + t, 1 - dz, 0, down_z, True)
        else:
            mine(0)
            others(0)

    even = chunk(0)[0]
    for a, (k, m) in enumerate(((THREE_DOWN + 2, FOUR_UP + 3), (THREE_UP + 2, FOUR_DOWN + 3))):
        whole = pack(0, a)
        for number, device in ((k, down_z), (m, up_z)):
            r_copy(number, device).wait_recv()
            whole = whole + landed[number].astype(jnp.float32)
        tails = whole[:, 768:896]
        turned = pltpu.roll(tails, 64, 1)
        for k in range(2):
            main = whole[:, k * 384 : (k + 1) * 384]
            lower, upper = (tails, turned) if k == 0 else (turned, tails)
            plain = jnp.concatenate([main, lower], axis=1)
            moved = pltpu.roll(jnp.concatenate([upper, main], axis=1), 448, 1)
            final[pl.ds(a * SLAB + k * 64, 64), :] = jnp.where(even, plain, moved)
    out_ref[...] = jnp.transpose(final[...])[0:FEAT].astype(jnp.bfloat16)

    for copy in own_sends:
        copy.wait_send()
    for h in range(2):
        kv_copy(P_UP, cross, h, up_x).wait_send()
        kv_copy(P_DOWN, cross, h, down_x).wait_send()
        kv_copy(FAR_P, far, h, across).wait_send()
        part_copy(FAR_UP, low, h, 0, up_x).wait_send()
        part_copy(FAR_DOWN, high, h, 1, down_x).wait_send()
        for k in range(1, 8):
            sib_copy(k, blocks[k], h).wait_send()
    for g in range(4):
        for copy in (w_beside(g), w_across(g), w_up(g), w_down(g)):
            copy.wait_send()
        for i in range(4):
            w_sib(i, g).wait_send()
    for a in range(2):
        o_copy(a).wait_send()
    for k in range(14):
        r_copy(k, up_z).wait_send()


def shards(c_query, w_uq, w_uk, w_uv, w_out, kv_latent, slab_order, block_table):
    bf16 = jnp.bfloat16
    dma = pltpu.SemaphoreType.DMA
    turned = pl.pallas_call(
        kernel,
        out_shape=jax.ShapeDtypeStruct((FEAT, TOK), bf16),
        in_specs=[pl.BlockSpec(memory_space=pl.ANY)] * 6
        + [pl.BlockSpec(memory_space=pltpu.SMEM)] * 2,
        out_specs=pl.BlockSpec(memory_space=pltpu.VMEM),
        scratch_shapes=[
            pltpu.VMEM((TOK, QR), bf16),
            pltpu.VMEM((QR, HEADS * (NOPE + ROPE)), bf16),
            pltpu.VMEM((HEADS, NOPE, LAT), bf16),
            pltpu.VMEM((HEADS, LAT, VD), bf16),
            pltpu.VMEM((GROUP, SIDE), bf16),
            pltpu.VMEM((GROUP, SIDE), bf16),
            pltpu.VMEM((32, KEY, SLAB), bf16),
            pltpu.VMEM((2, HEADS * SLAB, KEY), bf16),
            pltpu.VMEM((2, HEADS * SLAB, LAT), jnp.float32),
            pltpu.VMEM((2, HEADS * SLAB, 128), jnp.float32),
            pltpu.VMEM((2, HEADS * SLAB, 128), jnp.float32),
            pltpu.VMEM((TOK, GROUP), bf16),
            pltpu.VMEM((TOK, GROUP), bf16),
            pltpu.VMEM((14, 64, PAIR), bf16),
            pltpu.VMEM((14, 64, PAIR), bf16),
            pltpu.VMEM((TOK, WINDOW), jnp.float32),
            pltpu.VMEM((NZ, TOK, WINDOW), jnp.float32),
            dma((7,)),
            dma((N_KV,)),
            dma((N_KV,)),
            dma((8, 4)),
            dma((8, 4)),
            dma((2,)),
            dma((2,)),
            dma((14,)),
            dma((14,)),
        ],
        compiler_params=pltpu.CompilerParams(
            collective_id=0, has_side_effects=True, vmem_limit_bytes=58 * 2**20
        ),
        name="attention",
    )(c_query, w_uq, w_uk, w_uv, w_out, kv_latent.T, slab_order, block_table)
    return turned.T


def solution(mesh):
    in_specs = (
        P("ctx", None),
        P(None, "tp"),
        P("tp", None, None),
        P("tp", None, None),
        P("tp", None),
        P("ctx", None),
        P(),
        P(),
    )
    return jax.shard_map(
        shards, mesh=mesh, in_specs=in_specs, out_specs=P("ctx", "tp"), check_vma=False
    )
```

```python
import jax
import jax.numpy as jnp
import numpy as np
from jax import lax
from jax.experimental import pallas as pl
from jax.experimental.pallas import tpu as pltpu
from jax.sharding import PartitionSpec as P

MESH = pl.DeviceIdType.MESH
SLAB = 128
TOK = 256
HALF = TOK // 2
HEADS = 4
NOPE = 128
ROPE = 64
LAT = 512
KEY = LAT + ROPE
QR = 1536
VD = 128
GROUP = HEADS * VD
FEAT = 448
NZ = 8
SIDE = NZ * FEAT
WINDOW = 512
PAIR = 2 * FEAT
SCALE = float((NOPE + ROPE) ** -0.5 * np.log2(np.e))
FILL = -1e30

N_KV = 48
WHOLE, UPPER, LOWER = (0, KEY), (0, KEY // 2), (KEY // 2, KEY // 2)


def dot(a, b):
    return jnp.dot(a, b, preferred_element_type=jnp.float32)


def kernel(
    cq_hbm, wuq_hbm, wuk_hbm, wuv_hbm, wout_hbm, kv_hbm, order_ref, table_ref,
    out_ref,
    cq, wuq, wuk, wuv, wown, woth, kvbuf, qbuf, acc, top, den, oown, ooth, packed, landed, parts,
    load_sem, kv_send, kv_recv, w_send, w_recv, o_send, o_recv, r_send, r_recv,
):
    ctx = lax.axis_index("ctx")
    tp = lax.axis_index("tp")
    core = lax.rem(ctx, 2)
    yh = lax.rem(lax.div(ctx, 2), 2)
    x = lax.div(ctx, 4)
    yl = lax.div(tp, NZ)
    z = lax.rem(tp, NZ)

    def at(dx, flip_h, flip_l, dz, flip_core):
        nx = lax.rem(x + dx + 4, 4)
        nh = 1 - yh if flip_h else yh
        nl = 1 - yl if flip_l else yl
        nz = lax.rem(z + dz + NZ, NZ)
        nc = 1 - core if flip_core else core
        return ((nx * 2 + nh) * 2 + nc, nl * NZ + nz)

    up_x, down_x = at(1, 0, 0, 0, 0), at(-1, 0, 0, 0, 0)
    across, beside = at(0, 1, 1, 0, 0), at(0, 0, 1, 0, 0)
    up_z, down_z = at(0, 0, 0, 1, 0), at(0, 0, 0, -1, 0)
    sibling = at(0, 0, 0, 0, 1)

    def block(dx, flip_h, flip_core):
        return at(dx, flip_h, 0, 0, flip_core)[0]

    loads = [
        pltpu.make_async_copy(cq_hbm, cq, load_sem.at[0]),
        pltpu.make_async_copy(wuq_hbm, wuq, load_sem.at[1]),
        pltpu.make_async_copy(wuk_hbm, wuk, load_sem.at[2]),
        pltpu.make_async_copy(kv_hbm.at[:, 0:SLAB], kvbuf.at[2 * ctx], load_sem.at[3]),
        pltpu.make_async_copy(wuv_hbm, wuv, load_sem.at[4]),
        pltpu.make_async_copy(
            wout_hbm.at[:, pl.ds(pl.multiple_of(yl * SIDE, 128), SIDE)], wown, load_sem.at[5]
        ),
        pltpu.make_async_copy(kv_hbm.at[:, SLAB:TOK], kvbuf.at[2 * ctx + 1], load_sem.at[6]),
    ]
    for load in loads:
        load.start()

    barrier = pltpu.get_barrier_semaphore()
    for device in (up_x, down_x, across, beside, up_z, down_z, sibling):
        pl.semaphore_signal(barrier, inc=1, device_id=device, device_id_type=MESH)
    pl.semaphore_wait(barrier, 7)

    here = lax.rem(z, 2)
    there = 1 - here
    targets = {
        "up_x": up_x, "down_x": down_x, "across": across, "up_z": up_z, "down_z": down_z, "sibling": sibling,
    }
    places = {
        "own": (0, 0), "low": (-1, 0), "high": (1, 0), "cross": (0, 1),
        "far": (2, 0), "low_cross": (-1, 1), "high_cross": (1, 1), "far_cross": (2, 1),
    }
    blocks = {name: block(dx, flip, 0) for name, (dx, flip) in places.items()}
    sib_blocks = {name: block(dx, flip, 1) for name, (dx, flip) in places.items()}
    numbers, sent = {}, []

    def kv_copy(tag, name, h, rows, target, theirs=False):
        number = numbers.setdefault(tag, len(numbers))
        slab = 2 * (sib_blocks if theirs else blocks)[name] + h
        part = pl.ds(*rows)
        source = kvbuf.at[slab, part]
        if name == "own":
            source = kv_hbm.at[part, pl.ds(pl.multiple_of(h * SLAB, SLAB), SLAB)]
        return pltpu.make_async_remote_copy(
            src_ref=source,
            dst_ref=kvbuf.at[slab, part],
            send_sem=kv_send.at[number],
            recv_sem=kv_recv.at[number],
            device_id=targets[target],
            device_id_type=MESH,
        )

    def give(tag, name, h, target, rows=WHOLE):
        sent.append((tag, name, h, rows, target))
        kv_copy(tag, name, h, rows, target).start()

    def take(tag, name, h, rows=WHOLE):
        kv_copy(tag, name, h, rows, "sibling").wait_recv()

    def is_here(h):
        return "h" if h is here else "t"

    def share(names, h):
        for name in names:
            give("s" + name + is_here(h), name, h, "sibling")

    def land(names, h):
        for name in names:
            kv_copy("s" + name + is_here(h), name, h, WHOLE, "sibling", True).wait_recv()

    for tag, rows in (("u", UPPER), ("l", LOWER)):
        for target in ("up_x", "down_x", "across"):
            give(target + tag, "own", here, target, rows)
    give("across", "own", there, "across")
    share(["own"], here)
    share(["own"], there)

    def group_columns(g):
        base = lax.div(z, 2)
        steps = (2, 1 - 2 * lax.rem(z, 2), 2 * lax.rem(z, 2) - 1, 0)
        return lax.rem(base + steps[g] + 4, 4) * PAIR

    def quarter(dx, dc):
        return lax.rem(x + dx + 4, 4) * 128 + (1 - core if dc else core) * 64

    def w_copy(index, src, src_base, r, n, g, device):
        cols = group_columns(g)
        return pltpu.make_async_remote_copy(
            src_ref=src.at[pl.ds(r, n), pl.ds(pl.multiple_of(src_base + cols, 128), PAIR)],
            dst_ref=woth.at[pl.ds(r, n), pl.ds(pl.multiple_of(cols, 128), PAIR)],
            send_sem=w_send.at[index, g],
            recv_sem=w_recv.at[index, g],
            device_id=device,
            device_id_type=MESH,
        )

    other = (1 - yl) * SIDE
    w_dx = (0, 2, 1, -1)

    def w_beside(k, g):
        return w_copy(k, wout_hbm, other, quarter(w_dx[k], 0), 64, g, beside)

    def w_across(g):
        return w_copy(2, wout_hbm, other, quarter(1, 0), 64, g, across)

    def w_up(g):
        return w_copy(3, woth, 0, quarter(0, 0), 32, g, up_x)

    def w_down(g):
        return w_copy(4, woth, 0, quarter(2, 0) + 32, 32, g, down_x)

    def w_landed(k, g):
        if k < 3:
            return w_copy(k, woth, 0, quarter(w_dx[k], 0), 64, g, sibling)
        if k < 5:
            return w_copy(k, woth, 0, quarter(-1, 0) + 32 * (k - 3), 32, g, sibling)
        return w_copy(k, woth, 0, quarter(w_dx[k - 5], 1), 64, g, sibling)

    def w_sib(k, g):
        return w_copy(5 + k, woth, 0, quarter(w_dx[k], 0), 64, g, sibling)

    def pass_on(g):
        for k in range(2):
            w_landed(k, g).wait_recv()
            w_sib(k, g).start()
        w_up(g).start()
        w_down(g).start()

    for g in range(4):
        for k in range(2):
            w_beside(k, g).start()

    lane = lax.broadcasted_iota(jnp.int32, (SLAB, 128), 1)
    row = lax.broadcasted_iota(jnp.int32, (SLAB, 128), 0)
    delta = lane - row
    seqs = [order_ref[2 * ctx + a] for a in range(2)]
    loads[0].wait()
    loads[1].wait()
    loads[2].wait()
    first_half = lax.rem(lane, 64) < 32
    freq = jnp.exp(lax.rem(lane, 32).astype(jnp.float32) * float(-np.log(10000.0) / 32))
    for a in range(2):
        pos = (seqs[a] * SLAB + row).astype(jnp.float32)
        angle = pos * freq
        cosine = jnp.cos(angle) * SCALE
        sine = jnp.sin(angle) * SCALE
        sine = jnp.where(first_half, -sine, sine)
        rows_a = pl.ds(a * SLAB, SLAB)
        for k in range(2):
            q = dot(cq[rows_a, :], wuq[:, k * 384 : (k + 1) * 384])
            shifted = pltpu.roll(q, 64, 1)
            nopes = (q[:, 0:128], shifted[:, 256:384])
            pair = jnp.where(lane < 64, q[:, 128:256], q[:, 256:384])
            swapped = jnp.where(first_half, pltpu.roll(pair, 96, 1), pltpu.roll(pair, 32, 1))
            turned = pair * cosine + swapped * sine
            ropes = (turned, pltpu.roll(turned, 64, 1))
            for j in range(2):
                h = 2 * k + j
                q_lat = dot(nopes[j].astype(jnp.bfloat16), wuk[h]) * SCALE
                for u in range(2):
                    rows_h = pl.ds((a * HEADS + h) * 64, 64)
                    half = slice(u * 64, u * 64 + 64)
                    qbuf[u, rows_h, 0:LAT] = q_lat[half].astype(jnp.bfloat16)
                    qbuf[u, rows_h, LAT:KEY] = ropes[j][half, 0:ROPE].astype(jnp.bfloat16)

    top[...] = jnp.full_like(top, FILL)
    den[...] = jnp.zeros_like(den)
    acc[...] = jnp.zeros_like(acc)

    def scores(u, keys):
        return dot(qbuf[u], keys)

    def absorb(u, slabs, keys, score):
        width = len(slabs) * SLAB
        biases = []
        for a in range(2):
            bias = []
            for slab in slabs:
                seq_k = order_ref[slab]
                allowed = table_ref[seqs[a], seq_k] == 1
                limit = jnp.where(seq_k < seqs[a], SLAB, jnp.where(seq_k == seqs[a], 0, -SLAB))
                limit = jnp.where(allowed, limit, -SLAB)
                bias.append(jnp.where(delta[u * 64 : u * 64 + 64] <= limit, 0.0, FILL))
            biases.append(jnp.concatenate(bias, axis=1))
        bias = jnp.stack(biases)
        score = (score.reshape(2, HEADS, 64, width) + bias[:, None]).reshape(2 * HEADS * 64, width)
        old = top[u]
        new = jnp.maximum(old, jnp.max(score, axis=1, keepdims=True))
        top[u] = new
        shrink = jnp.exp2(old - new)
        weight = jnp.exp2(score - new[:, 0:1])
        part = weight[:, 0:128]
        for k in range(1, len(slabs)):
            part = part + weight[:, k * 128 : (k + 1) * 128]
        den[u] = den[u] * shrink + part
        mixed = lax.dot_general(
            weight.astype(jnp.bfloat16),
            keys[0:LAT],
            (((1,), (1,)), ((), ())),
            preferred_element_type=jnp.float32,
        )
        acc[u] = acc[u] * shrink[:, 0:1] + mixed

    def attend(slabs, last=False):
        keys = jnp.concatenate([kvbuf[slab] for slab in slabs], axis=1)
        first, second = scores(0, keys), scores(1, keys)
        absorb(0, slabs, keys, first)
        if last:
            finish(0)
            o_copy(0).start()
        absorb(1, slabs, keys, second)
        if last:
            finish(1)
            o_copy(1).start()

    def finish(u):
        total = jnp.sum(den[u], axis=1, keepdims=True)
        o_lat = (acc[u] / total).astype(jnp.bfloat16).reshape(2, HEADS, 64, LAT)
        for h in range(HEADS):
            o_head = dot(o_lat[:, h].reshape(SLAB, LAT), wuv[h])
            oown[pl.ds(u * SLAB, SLAB), h * VD : (h + 1) * VD] = o_head.astype(jnp.bfloat16)

    def o_copy(a):
        part = pl.ds(a * SLAB, SLAB)
        return pltpu.make_async_remote_copy(
            src_ref=oown.at[part],
            dst_ref=ooth.at[part],
            send_sem=o_send.at[a],
            recv_sem=o_recv.at[a],
            device_id=beside,
            device_id_type=MESH,
        )

    near = ["low", "high", "cross"]
    later = ["far", "low_cross", "high_cross"]

    def step(i, carry):
        @pl.when(i == 0)
        def _():
            take("up_xu", "low", here, UPPER)
            give("far_u", "low", here, "up_x", UPPER)
            take("acrossu", "cross", here, UPPER)
            give("cross_du", "cross", here, "down_x", UPPER)
            give("cross_uu", "cross", here, "up_x", UPPER)
            take("down_xu", "high", here, UPPER)
            take("down_xl", "high", here, LOWER)
            give("far_l", "high", here, "down_x", LOWER)
            take("acrossl", "cross", here, LOWER)
            give("cross_dl", "cross", here, "down_x", LOWER)
            give("cross_ul", "cross", here, "up_x", LOWER)
            give("up_x", "own", there, "up_x")
            give("down_x", "own", there, "down_x")
            take("up_xl", "low", here, LOWER)
            share(near, here)
            loads[3].wait()
            loads[6].wait()
            land(["own"], here)
            land(["own"], there)

        @pl.when(i == 1)
        def _():
            take("far_u", "far", here, UPPER)
            give("far_cross_u", "far", here, "across", UPPER)
            give("z_far_u", "far", here, "up_z", UPPER)
            take("far_l", "far", here, LOWER)
            give("far_cross_l", "far", here, "across", LOWER)
            give("z_far_l", "far", here, "down_z", LOWER)
            share(["far"], here)
            take("cross_du", "high_cross", here, UPPER)
            give("z_high_u", "high_cross", here, "up_z", UPPER)
            take("cross_uu", "low_cross", here, UPPER)
            give("z_low_u", "low_cross", here, "up_z", UPPER)
            take("cross_dl", "high_cross", here, LOWER)
            give("z_high_l", "high_cross", here, "down_z", LOWER)
            take("cross_ul", "low_cross", here, LOWER)
            give("z_low_l", "low_cross", here, "down_z", LOWER)
            share(["high_cross", "low_cross"], here)
            land(near, here)

        @pl.when(i == 2)
        def _():
            take("across", "cross", there)
            share(["cross"], there)
            take("far_cross_u", "far_cross", here, UPPER)
            give("z_fc_u", "far_cross", here, "up_z", UPPER)
            take("far_cross_l", "far_cross", here, LOWER)
            give("z_fc_l", "far_cross", here, "down_z", LOWER)
            share(["far_cross"], here)
            for g in range(4):
                w_across(g).start()
            take("up_x", "low", there)
            take("down_x", "high", there)
            share(["low", "high"], there)
            land(later, here)

        @pl.when(i == 3)
        def _():
            take("z_far_u", "far", there, UPPER)
            take("z_far_l", "far", there, LOWER)
            share(["far"], there)
            take("z_high_u", "high_cross", there, UPPER)
            take("z_high_l", "high_cross", there, LOWER)
            share(["high_cross"], there)
            take("z_low_u", "low_cross", there, UPPER)
            take("z_low_l", "low_cross", there, LOWER)
            share(["low_cross"], there)
            land(near, there)
            for g in range(2):
                pass_on(g)

        @pl.when(i == 4)
        def _():
            take("z_fc_u", "far_cross", there, UPPER)
            take("z_fc_l", "far_cross", there, LOWER)
            share(["far_cross"], there)
            land(later, there)

        @pl.when(i == 5)
        def _():
            for g in range(2, 4):
                pass_on(g)
            land(["far_cross"], here)
            land(["far_cross"], there)

        def slabs(names, h):
            return [2 * of[name] + h for name in names for of in (blocks, sib_blocks)]

        def pick(choices):
            chosen = choices[0]
            for k, choice in enumerate(choices[1:]):
                chosen = [jnp.where(i == k + 2, b, a) for a, b in zip(chosen, choice)]
            return chosen

        @pl.when(i == 0)
        def _():
            attend(slabs(["own"], 0) + slabs(["own"], 1))

        @pl.when((i > 0) & (i < 5))
        def _():
            attend(pick([slabs(near, here), slabs(later, here), slabs(near, there), slabs(later, there)]))

        @pl.when(i == 5)
        def _():
            loads[4].wait()
            attend(slabs(["far_cross"], 0) + slabs(["far_cross"], 1), True)

        return carry

    lax.fori_loop(0, 6, step, 0)
    loads[5].wait()

    lane32 = lax.broadcasted_iota(jnp.int32, (32, 128), 1)
    FOUR_UP, FOUR_DOWN, THREE_UP, THREE_DOWN = 0, 4, 8, 11

    def r_copy(k, u, device):
        return pltpu.make_async_remote_copy(
            src_ref=packed.at[k, u],
            dst_ref=landed.at[k, u],
            send_sem=r_send.at[k, u],
            recv_sem=r_recv.at[k, u],
            device_id=device,
            device_id_type=MESH,
        )

    def chunk(dz):
        d = lax.rem(z + dz + NZ, NZ)
        odd = lax.rem(d, 2)
        return odd == 0, pl.ds(pl.multiple_of(d * FEAT - odd * 64, 128), WINDOW)

    def mine(dz):
        parts[dz % NZ] = dot(oown[...], wown[:, chunk(dz)[1]])

    def others(dz, u=None):
        rows_u = pl.ds(0, TOK) if u is None else pl.ds(u * SLAB, SLAB)
        parts[dz % NZ, rows_u] += dot(ooth[rows_u, :], woth[:, chunk(dz)[1]])

    def pack(dz, a, u):
        even = chunk(dz)[0]
        part = parts[dz % NZ, pl.ds(u * SLAB + a * 64, 64)]
        main = jnp.where(even, part[:, 0:384], part[:, 128:512])
        tail = jnp.where(even, part[:, 384:512], part[:, 0:128])
        first, second = tail[0:32], tail[32:64]
        tails = jnp.where(
            even,
            jnp.where(lane32 < 64, first, pltpu.roll(second, 64, 1)),
            jnp.where(lane32 < 64, pltpu.roll(first, 64, 1), second),
        )
        return jnp.concatenate([main[0:32], main[32:64], tails], axis=1)

    def send(k, dz, a, u, device, follows):
        total = pack(dz, a, u)
        if follows:
            r_copy(k - 1, u, device).wait_recv()
            total = total + landed[k - 1, u].astype(jnp.float32)
        packed[k, u] = total.astype(jnp.bfloat16)
        r_copy(k, u, device).start()

    def land_group(g):
        w_landed(2, g).wait_recv()
        w_sib(2, g).start()
        for k in (3, 4):
            w_landed(k, g).wait_recv()
        w_sib(3, g).start()
        for k in range(5, 9):
            w_landed(k, g).wait_recv()

    for dz in (4, 3, -3):
        mine(dz)
    land_group(0)
    land_group(1)
    for u in range(2):
        o_copy(u).wait_recv()
        others(4, u)
        send(FOUR_UP, 4, 0, u, up_z, False)
        send(FOUR_DOWN, 4, 1, u, down_z, False)
        for dz in (3, -3):
            others(dz, u)
        send(THREE_UP, 3, 1, u, up_z, False)
        send(THREE_DOWN, -3, 0, u, down_z, False)
    for t in range(1, 4):
        dz = 4 - t
        for u in range(2):
            send(FOUR_UP + t, dz, 0, u, up_z, True)
            send(FOUR_DOWN + t, -dz, 1, u, down_z, True)
        if t < 3:
            land_group(t + 1)
            for nearer in (dz - 1, 1 - dz):
                mine(nearer)
                others(nearer)
            for u in range(2):
                send(THREE_UP + t, dz - 1, 1, u, up_z, True)
                send(THREE_DOWN + t, 1 - dz, 0, u, down_z, True)
        else:
            mine(0)
            others(0)

    even = chunk(0)[0]
    for u in range(2):
        for a, (n, m) in enumerate(((THREE_DOWN + 2, FOUR_UP + 3), (THREE_UP + 2, FOUR_DOWN + 3))):
            whole = pack(0, a, u)
            for number, device in ((n, down_z), (m, up_z)):
                r_copy(number, u, device).wait_recv()
                whole = whole + landed[number, u].astype(jnp.float32)
            tails = whole[:, 768:896]
            turned = pltpu.roll(tails, 64, 1)
            for k in range(2):
                main = whole[:, k * 384 : (k + 1) * 384]
                lower, upper = (tails, turned) if k == 0 else (turned, tails)
                plain = jnp.concatenate([main, lower], axis=1)
                moved = pltpu.roll(jnp.concatenate([upper, main], axis=1), 448, 1)
                result = jnp.where(even, plain, moved)[:, 0:FEAT]
                out_ref[pl.ds(a * SLAB + u * 64 + k * 32, 32), :] = result.astype(jnp.bfloat16)

    for tag, name, h, rows, target in sent:
        kv_copy(tag, name, h, rows, target).wait_send()
    for g in range(4):
        for copy in (w_beside(0, g), w_beside(1, g), w_across(g), w_up(g), w_down(g)):
            copy.wait_send()
        for i in range(4):
            w_sib(i, g).wait_send()
    for u in range(2):
        o_copy(u).wait_send()
    for k in range(14):
        for u in range(2):
            r_copy(k, u, up_z).wait_send()


def shards(c_query, w_uq, w_uk, w_uv, w_out, kv_latent, slab_order, block_table):
    bf16 = jnp.bfloat16
    dma = pltpu.SemaphoreType.DMA
    return pl.pallas_call(
        kernel,
        out_shape=jax.ShapeDtypeStruct((TOK, FEAT), bf16),
        in_specs=[pl.BlockSpec(memory_space=pl.ANY)] * 6
        + [pl.BlockSpec(memory_space=pltpu.SMEM)] * 2,
        out_specs=pl.BlockSpec(memory_space=pltpu.VMEM),
        scratch_shapes=[
            pltpu.VMEM((TOK, QR), bf16),
            pltpu.VMEM((QR, HEADS * (NOPE + ROPE)), bf16),
            pltpu.VMEM((HEADS, NOPE, LAT), bf16),
            pltpu.VMEM((HEADS, LAT, VD), bf16),
            pltpu.VMEM((GROUP, SIDE), bf16),
            pltpu.VMEM((GROUP, SIDE), bf16),
            pltpu.VMEM((32, KEY, SLAB), bf16),
            pltpu.VMEM((2, HEADS * SLAB, KEY), bf16),
            pltpu.VMEM((2, HEADS * SLAB, LAT), jnp.float32),
            pltpu.VMEM((2, HEADS * SLAB, 128), jnp.float32),
            pltpu.VMEM((2, HEADS * SLAB, 128), jnp.float32),
            pltpu.VMEM((TOK, GROUP), bf16),
            pltpu.VMEM((TOK, GROUP), bf16),
            pltpu.VMEM((14, 2, 32, PAIR), bf16),
            pltpu.VMEM((14, 2, 32, PAIR), bf16),
            pltpu.VMEM((NZ, TOK, WINDOW), jnp.float32),
            dma((7,)),
            dma((N_KV,)),
            dma((N_KV,)),
            dma((9, 4)),
            dma((9, 4)),
            dma((2,)),
            dma((2,)),
            dma((14, 2)),
            dma((14, 2)),
        ],
        compiler_params=pltpu.CompilerParams(
            collective_id=0, has_side_effects=True, vmem_limit_bytes=58 * 2**20
        ),
        name="attention",
    )(c_query, w_uq, w_uk, w_uv, w_out, kv_latent.T, slab_order, block_table)


def solution(mesh):
    in_specs = (
        P("ctx", None),
        P(None, "tp"),
        P("tp", None, None),
        P("tp", None, None),
        P("tp", None),
        P("ctx", None),
        P(),
        P(),
    )
    return jax.shard_map(
        shards, mesh=mesh, in_specs=in_specs, out_specs=P("ctx", "tp"), check_vma=False
    )
```

```python
import jax
import jax.numpy as jnp
import numpy as np
from jax import lax
from jax.experimental import pallas as pl
from jax.experimental.pallas import tpu as pltpu
from jax.sharding import PartitionSpec as P

MESH = pl.DeviceIdType.MESH
SLAB = 128
TOK = 256
HALF = TOK // 2
HEADS = 4
NOPE = 128
ROPE = 64
LAT = 512
KEY = LAT + ROPE
QR = 1536
VD = 128
GROUP = HEADS * VD
FEAT = 448
NZ = 8
SIDE = NZ * FEAT
WINDOW = 512
PAIR = 2 * FEAT
SCALE = float((NOPE + ROPE) ** -0.5 * np.log2(np.e))
FILL = -1e30

N_KV = 48
WHOLE, UPPER, LOWER = (0, KEY), (0, KEY // 2), (KEY // 2, KEY // 2)


def dot(a, b):
    return jnp.dot(a, b, preferred_element_type=jnp.float32)


def kernel(
    cq_hbm, wuq_hbm, wuk_hbm, wuv_hbm, wout_hbm, kv_hbm, order_ref, table_ref,
    out_ref,
    cq, wuq, wuk, wuv, wown, woth, kvbuf, qbuf, acc, top, den, oown, ooth, packed, landed, parts,
    load_sem, kv_send, kv_recv, w_send, w_recv, o_send, o_recv, r_send, r_recv,
):
    ctx = lax.axis_index("ctx")
    tp = lax.axis_index("tp")
    core = lax.rem(ctx, 2)
    yh = lax.rem(lax.div(ctx, 2), 2)
    x = lax.div(ctx, 4)
    yl = lax.div(tp, NZ)
    z = lax.rem(tp, NZ)

    def at(dx, flip_h, flip_l, dz, flip_core):
        nx = lax.rem(x + dx + 4, 4)
        nh = 1 - yh if flip_h else yh
        nl = 1 - yl if flip_l else yl
        nz = lax.rem(z + dz + NZ, NZ)
        nc = 1 - core if flip_core else core
        return ((nx * 2 + nh) * 2 + nc, nl * NZ + nz)

    up_x, down_x = at(1, 0, 0, 0, 0), at(-1, 0, 0, 0, 0)
    across, beside = at(0, 1, 1, 0, 0), at(0, 0, 1, 0, 0)
    up_z, down_z = at(0, 0, 0, 1, 0), at(0, 0, 0, -1, 0)
    sibling = at(0, 0, 0, 0, 1)

    def block(dx, flip_h, flip_core):
        return at(dx, flip_h, 0, 0, flip_core)[0]

    loads = [
        pltpu.make_async_copy(cq_hbm, cq, load_sem.at[0]),
        pltpu.make_async_copy(wuq_hbm, wuq, load_sem.at[1]),
        pltpu.make_async_copy(wuk_hbm, wuk, load_sem.at[2]),
        pltpu.make_async_copy(kv_hbm.at[:, 0:SLAB], kvbuf.at[2 * ctx], load_sem.at[3]),
        pltpu.make_async_copy(wuv_hbm, wuv, load_sem.at[4]),
        pltpu.make_async_copy(
            wout_hbm.at[:, pl.ds(pl.multiple_of(yl * SIDE, 128), SIDE)], wown, load_sem.at[5]
        ),
        pltpu.make_async_copy(kv_hbm.at[:, SLAB:TOK], kvbuf.at[2 * ctx + 1], load_sem.at[6]),
    ]
    for load in loads:
        load.start()

    barrier = pltpu.get_barrier_semaphore()
    for device in (up_x, down_x, across, beside, up_z, down_z, sibling):
        pl.semaphore_signal(barrier, inc=1, device_id=device, device_id_type=MESH)
    pl.semaphore_wait(barrier, 7)

    here = lax.rem(z, 2)
    there = 1 - here
    targets = {
        "up_x": up_x, "down_x": down_x, "across": across, "up_z": up_z, "down_z": down_z, "sibling": sibling,
    }
    places = {
        "own": (0, 0), "low": (-1, 0), "high": (1, 0), "cross": (0, 1),
        "far": (2, 0), "low_cross": (-1, 1), "high_cross": (1, 1), "far_cross": (2, 1),
    }
    blocks = {name: block(dx, flip, 0) for name, (dx, flip) in places.items()}
    sib_blocks = {name: block(dx, flip, 1) for name, (dx, flip) in places.items()}
    numbers, sent = {}, []

    def kv_copy(tag, name, h, rows, target, theirs=False):
        number = numbers.setdefault(tag, len(numbers))
        slab = 2 * (sib_blocks if theirs else blocks)[name] + h
        part = pl.ds(*rows)
        source = kvbuf.at[slab, part]
        if name == "own":
            source = kv_hbm.at[part, pl.ds(pl.multiple_of(h * SLAB, SLAB), SLAB)]
        return pltpu.make_async_remote_copy(
            src_ref=source,
            dst_ref=kvbuf.at[slab, part],
            send_sem=kv_send.at[number],
            recv_sem=kv_recv.at[number],
            device_id=targets[target],
            device_id_type=MESH,
        )

    def give(tag, name, h, target, rows=WHOLE):
        sent.append((tag, name, h, rows, target))
        kv_copy(tag, name, h, rows, target).start()

    def take(tag, name, h, rows=WHOLE):
        kv_copy(tag, name, h, rows, "sibling").wait_recv()

    def is_here(h):
        return "h" if h is here else "t"

    def share(names, h):
        for name in names:
            give("s" + name + is_here(h), name, h, "sibling")

    def land(names, h):
        for name in names:
            kv_copy("s" + name + is_here(h), name, h, WHOLE, "sibling", True).wait_recv()

    for tag, rows in (("u", UPPER), ("l", LOWER)):
        for target in ("up_x", "down_x", "across"):
            give(target + tag, "own", here, target, rows)
    give("across", "own", there, "across")
    share(["own"], here)
    share(["own"], there)

    def group_columns(g):
        base = lax.div(z, 2)
        steps = (2, 1 - 2 * lax.rem(z, 2), 2 * lax.rem(z, 2) - 1, 0)
        return lax.rem(base + steps[g] + 4, 4) * PAIR

    def quarter(dx, dc):
        return lax.rem(x + dx + 4, 4) * 128 + (1 - core if dc else core) * 64

    def w_copy(index, src, src_base, r, n, g, device):
        cols = group_columns(g)
        return pltpu.make_async_remote_copy(
            src_ref=src.at[pl.ds(r, n), pl.ds(pl.multiple_of(src_base + cols, 128), PAIR)],
            dst_ref=woth.at[pl.ds(r, n), pl.ds(pl.multiple_of(cols, 128), PAIR)],
            send_sem=w_send.at[index, g],
            recv_sem=w_recv.at[index, g],
            device_id=device,
            device_id_type=MESH,
        )

    other = (1 - yl) * SIDE
    w_dx = (0, 2, 1, -1)

    def w_beside(k, g):
        return w_copy(k, wout_hbm, other, quarter(w_dx[k], 0), 64, g, beside)

    def w_across(g):
        return w_copy(2, wout_hbm, other, quarter(1, 0), 64, g, across)

    def w_up(g):
        return w_copy(3, woth, 0, quarter(0, 0), 32, g, up_x)

    def w_down(g):
        return w_copy(4, woth, 0, quarter(2, 0) + 32, 32, g, down_x)

    def w_landed(k, g):
        if k < 3:
            return w_copy(k, woth, 0, quarter(w_dx[k], 0), 64, g, sibling)
        if k < 5:
            return w_copy(k, woth, 0, quarter(-1, 0) + 32 * (k - 3), 32, g, sibling)
        return w_copy(k, woth, 0, quarter(w_dx[k - 5], 1), 64, g, sibling)

    def w_sib(k, g):
        return w_copy(5 + k, woth, 0, quarter(w_dx[k], 0), 64, g, sibling)

    def relay(g):
        w_landed(2, g).wait_recv()
        w_sib(2, g).start()
        for k in (3, 4):
            w_landed(k, g).wait_recv()
        w_sib(3, g).start()

    def settle(g):
        for k in range(5, 9):
            w_landed(k, g).wait_recv()

    def pass_on(g):
        for k in range(2):
            w_landed(k, g).wait_recv()
            w_sib(k, g).start()
        w_up(g).start()
        w_down(g).start()

    for g in range(4):
        for k in range(2):
            w_beside(k, g).start()

    lane = lax.broadcasted_iota(jnp.int32, (SLAB, 128), 1)
    row = lax.broadcasted_iota(jnp.int32, (SLAB, 128), 0)
    delta = lane - row
    seqs = [order_ref[2 * ctx + a] for a in range(2)]
    loads[0].wait()
    loads[1].wait()
    loads[2].wait()
    first_half = lax.rem(lane, 64) < 32
    freq = jnp.exp(lax.rem(lane, 32).astype(jnp.float32) * float(-np.log(10000.0) / 32))
    for a in range(2):
        pos = (seqs[a] * SLAB + row).astype(jnp.float32)
        angle = pos * freq
        cosine = jnp.cos(angle) * SCALE
        sine = jnp.sin(angle) * SCALE
        sine = jnp.where(first_half, -sine, sine)
        rows_a = pl.ds(a * SLAB, SLAB)
        for k in range(2):
            q = dot(cq[rows_a, :], wuq[:, k * 384 : (k + 1) * 384])
            shifted = pltpu.roll(q, 64, 1)
            nopes = (q[:, 0:128], shifted[:, 256:384])
            pair = jnp.where(lane < 64, q[:, 128:256], q[:, 256:384])
            swapped = jnp.where(first_half, pltpu.roll(pair, 96, 1), pltpu.roll(pair, 32, 1))
            turned = pair * cosine + swapped * sine
            ropes = (turned, pltpu.roll(turned, 64, 1))
            for j in range(2):
                h = 2 * k + j
                q_lat = dot(nopes[j].astype(jnp.bfloat16), wuk[h]) * SCALE
                for u in range(2):
                    rows_h = pl.ds((a * HEADS + h) * 64, 64)
                    half = slice(u * 64, u * 64 + 64)
                    qbuf[u, rows_h, 0:LAT] = q_lat[half].astype(jnp.bfloat16)
                    qbuf[u, rows_h, LAT:KEY] = ropes[j][half, 0:ROPE].astype(jnp.bfloat16)

    top[...] = jnp.full_like(top, FILL)
    den[...] = jnp.zeros_like(den)
    acc[...] = jnp.zeros_like(acc)

    def scores(u, keys):
        return dot(qbuf[u], keys)

    def absorb(u, slabs, keys, score):
        width = len(slabs) * SLAB
        biases = []
        for a in range(2):
            bias = []
            for slab in slabs:
                seq_k = order_ref[slab]
                allowed = table_ref[seqs[a], seq_k] == 1
                limit = jnp.where(seq_k < seqs[a], SLAB, jnp.where(seq_k == seqs[a], 0, -SLAB))
                limit = jnp.where(allowed, limit, -SLAB)
                bias.append(jnp.where(delta[u * 64 : u * 64 + 64] <= limit, 0.0, FILL))
            biases.append(jnp.concatenate(bias, axis=1))
        bias = jnp.stack(biases)
        score = (score.reshape(2, HEADS, 64, width) + bias[:, None]).reshape(2 * HEADS * 64, width)
        old = top[u]
        new = jnp.maximum(old, jnp.max(score, axis=1, keepdims=True))
        top[u] = new
        shrink = jnp.exp2(old - new)
        weight = jnp.exp2(score - new[:, 0:1])
        part = weight[:, 0:128]
        for k in range(1, len(slabs)):
            part = part + weight[:, k * 128 : (k + 1) * 128]
        den[u] = den[u] * shrink + part
        mixed = lax.dot_general(
            weight.astype(jnp.bfloat16),
            keys[0:LAT],
            (((1,), (1,)), ((), ())),
            preferred_element_type=jnp.float32,
        )
        acc[u] = acc[u] * shrink[:, 0:1] + mixed

    def attend(slabs, last=False):
        keys = jnp.concatenate([kvbuf[slab] for slab in slabs], axis=1)
        first, second = scores(0, keys), scores(1, keys)
        absorb(0, slabs, keys, first)
        if last:
            finish(0)
            o_copy(0).start()
        absorb(1, slabs, keys, second)
        if last:
            finish(1)
            o_copy(1).start()

    def finish(u):
        total = jnp.sum(den[u], axis=1, keepdims=True)
        o_lat = (acc[u] / total).astype(jnp.bfloat16).reshape(2, HEADS, 64, LAT)
        for h in range(HEADS):
            o_head = dot(o_lat[:, h].reshape(SLAB, LAT), wuv[h])
            oown[pl.ds(u * SLAB, SLAB), h * VD : (h + 1) * VD] = o_head.astype(jnp.bfloat16)

    def o_copy(a):
        part = pl.ds(a * SLAB, SLAB)
        return pltpu.make_async_remote_copy(
            src_ref=oown.at[part],
            dst_ref=ooth.at[part],
            send_sem=o_send.at[a],
            recv_sem=o_recv.at[a],
            device_id=beside,
            device_id_type=MESH,
        )

    near = ["low", "high", "cross"]
    later = ["far", "low_cross", "high_cross"]

    def step(i, carry):
        @pl.when(i == 0)
        def _():
            take("up_xu", "low", here, UPPER)
            give("far_u", "low", here, "up_x", UPPER)
            take("acrossu", "cross", here, UPPER)
            give("cross_du", "cross", here, "down_x", UPPER)
            give("cross_uu", "cross", here, "up_x", UPPER)
            take("down_xu", "high", here, UPPER)
            take("down_xl", "high", here, LOWER)
            give("far_l", "high", here, "down_x", LOWER)
            take("acrossl", "cross", here, LOWER)
            give("cross_dl", "cross", here, "down_x", LOWER)
            give("cross_ul", "cross", here, "up_x", LOWER)
            give("up_x", "own", there, "up_x")
            give("down_x", "own", there, "down_x")
            take("up_xl", "low", here, LOWER)
            share(near, here)
            loads[3].wait()
            loads[6].wait()
            land(["own"], here)
            land(["own"], there)

        @pl.when(i == 1)
        def _():
            take("far_u", "far", here, UPPER)
            give("far_cross_u", "far", here, "across", UPPER)
            give("z_far_u", "far", here, "up_z", UPPER)
            take("far_l", "far", here, LOWER)
            give("far_cross_l", "far", here, "across", LOWER)
            give("z_far_l", "far", here, "down_z", LOWER)
            share(["far"], here)
            take("cross_du", "high_cross", here, UPPER)
            give("z_high_u", "high_cross", here, "up_z", UPPER)
            take("cross_uu", "low_cross", here, UPPER)
            give("z_low_u", "low_cross", here, "up_z", UPPER)
            take("cross_dl", "high_cross", here, LOWER)
            give("z_high_l", "high_cross", here, "down_z", LOWER)
            take("cross_ul", "low_cross", here, LOWER)
            give("z_low_l", "low_cross", here, "down_z", LOWER)
            share(["high_cross", "low_cross"], here)
            land(near, here)

        @pl.when(i == 2)
        def _():
            take("across", "cross", there)
            share(["cross"], there)
            take("far_cross_u", "far_cross", here, UPPER)
            give("z_fc_u", "far_cross", here, "up_z", UPPER)
            take("far_cross_l", "far_cross", here, LOWER)
            give("z_fc_l", "far_cross", here, "down_z", LOWER)
            share(["far_cross"], here)
            for g in range(4):
                w_across(g).start()
            take("up_x", "low", there)
            take("down_x", "high", there)
            share(["low", "high"], there)
            land(later, here)

        @pl.when(i == 3)
        def _():
            take("z_far_u", "far", there, UPPER)
            take("z_far_l", "far", there, LOWER)
            share(["far"], there)
            take("z_high_u", "high_cross", there, UPPER)
            take("z_high_l", "high_cross", there, LOWER)
            share(["high_cross"], there)
            take("z_low_u", "low_cross", there, UPPER)
            take("z_low_l", "low_cross", there, LOWER)
            share(["low_cross"], there)
            land(near, there)
            for g in range(2):
                pass_on(g)

        @pl.when(i == 4)
        def _():
            take("z_fc_u", "far_cross", there, UPPER)
            take("z_fc_l", "far_cross", there, LOWER)
            share(["far_cross"], there)
            land(later, there)
            pass_on(2)

        @pl.when(i == 5)
        def _():
            pass_on(3)
            relay(0)
            relay(1)
            land(["far_cross"], here)
            land(["far_cross"], there)

        def slabs(names, h):
            return [2 * of[name] + h for name in names for of in (blocks, sib_blocks)]

        def pick(choices):
            chosen = choices[0]
            for k, choice in enumerate(choices[1:]):
                chosen = [jnp.where(i == k + 2, b, a) for a, b in zip(chosen, choice)]
            return chosen

        @pl.when(i == 0)
        def _():
            attend(slabs(["own"], 0) + slabs(["own"], 1))

        @pl.when((i > 0) & (i < 5))
        def _():
            attend(pick([slabs(near, here), slabs(later, here), slabs(near, there), slabs(later, there)]))

        @pl.when(i == 5)
        def _():
            loads[4].wait()
            attend(slabs(["far_cross"], 0) + slabs(["far_cross"], 1), True)

        return carry

    lax.fori_loop(0, 6, step, 0)
    loads[5].wait()

    lane32 = lax.broadcasted_iota(jnp.int32, (32, 128), 1)
    FOUR_UP, FOUR_DOWN, THREE_UP, THREE_DOWN = 0, 4, 8, 11

    def r_copy(k, u, device):
        return pltpu.make_async_remote_copy(
            src_ref=packed.at[k, u],
            dst_ref=landed.at[k, u],
            send_sem=r_send.at[k, u],
            recv_sem=r_recv.at[k, u],
            device_id=device,
            device_id_type=MESH,
        )

    def chunk(dz):
        d = lax.rem(z + dz + NZ, NZ)
        odd = lax.rem(d, 2)
        return odd == 0, pl.ds(pl.multiple_of(d * FEAT - odd * 64, 128), WINDOW)

    def mine(dz):
        parts[dz % NZ] = dot(oown[...], wown[:, chunk(dz)[1]])

    def others(dz, u=None):
        rows_u = pl.ds(0, TOK) if u is None else pl.ds(u * SLAB, SLAB)
        parts[dz % NZ, rows_u] += dot(ooth[rows_u, :], woth[:, chunk(dz)[1]])

    def pack(dz, a, u):
        even = chunk(dz)[0]
        part = parts[dz % NZ, pl.ds(u * SLAB + a * 64, 64)]
        main = jnp.where(even, part[:, 0:384], part[:, 128:512])
        tail = jnp.where(even, part[:, 384:512], part[:, 0:128])
        first, second = tail[0:32], tail[32:64]
        tails = jnp.where(
            even,
            jnp.where(lane32 < 64, first, pltpu.roll(second, 64, 1)),
            jnp.where(lane32 < 64, pltpu.roll(first, 64, 1), second),
        )
        return jnp.concatenate([main[0:32], main[32:64], tails], axis=1)

    def send(k, dz, a, u, device, follows):
        total = pack(dz, a, u)
        if follows:
            r_copy(k - 1, u, device).wait_recv()
            total = total + landed[k - 1, u].astype(jnp.float32)
        packed[k, u] = total.astype(jnp.bfloat16)
        r_copy(k, u, device).start()

    for dz in (4, 3, -3):
        mine(dz)
    settle(0)
    for u in range(2):
        o_copy(u).wait_recv()
        others(4, u)
        send(FOUR_UP, 4, 0, u, up_z, False)
        send(FOUR_DOWN, 4, 1, u, down_z, False)
        if u == 0:
            settle(1)
            relay(2)
        for dz in (3, -3):
            others(dz, u)
        send(THREE_UP, 3, 1, u, up_z, False)
        send(THREE_DOWN, -3, 0, u, down_z, False)
    for t in range(1, 4):
        dz = 4 - t
        for u in range(2):
            send(FOUR_UP + t, dz, 0, u, up_z, True)
            send(FOUR_DOWN + t, -dz, 1, u, down_z, True)
        if t < 3:
            if t == 1:
                relay(3)
            settle(t + 1)
            for nearer in (dz - 1, 1 - dz):
                mine(nearer)
                others(nearer)
            for u in range(2):
                send(THREE_UP + t, dz - 1, 1, u, up_z, True)
                send(THREE_DOWN + t, 1 - dz, 0, u, down_z, True)
        else:
            mine(0)
            others(0)

    even = chunk(0)[0]
    for u in range(2):
        for a, (n, m) in enumerate(((THREE_DOWN + 2, FOUR_UP + 3), (THREE_UP + 2, FOUR_DOWN + 3))):
            whole = pack(0, a, u)
            for number, device in ((n, down_z), (m, up_z)):
                r_copy(number, u, device).wait_recv()
                whole = whole + landed[number, u].astype(jnp.float32)
            tails = whole[:, 768:896]
            turned = pltpu.roll(tails, 64, 1)
            for k in range(2):
                main = whole[:, k * 384 : (k + 1) * 384]
                lower, upper = (tails, turned) if k == 0 else (turned, tails)
                plain = jnp.concatenate([main, lower], axis=1)
                moved = pltpu.roll(jnp.concatenate([upper, main], axis=1), 448, 1)
                result = jnp.where(even, plain, moved)[:, 0:FEAT]
                out_ref[pl.ds(a * SLAB + u * 64 + k * 32, 32), :] = result.astype(jnp.bfloat16)

    for tag, name, h, rows, target in sent:
        kv_copy(tag, name, h, rows, target).wait_send()
    for g in range(4):
        for copy in (w_beside(0, g), w_beside(1, g), w_across(g), w_up(g), w_down(g)):
            copy.wait_send()
        for i in range(4):
            w_sib(i, g).wait_send()
    for u in range(2):
        o_copy(u).wait_send()
    for k in range(14):
        for u in range(2):
            r_copy(k, u, up_z).wait_send()


def shards(c_query, w_uq, w_uk, w_uv, w_out, kv_latent, slab_order, block_table):
    bf16 = jnp.bfloat16
    dma = pltpu.SemaphoreType.DMA
    return pl.pallas_call(
        kernel,
        out_shape=jax.ShapeDtypeStruct((TOK, FEAT), bf16),
        in_specs=[pl.BlockSpec(memory_space=pl.ANY)] * 6
        + [pl.BlockSpec(memory_space=pltpu.SMEM)] * 2,
        out_specs=pl.BlockSpec(memory_space=pltpu.VMEM),
        scratch_shapes=[
            pltpu.VMEM((TOK, QR), bf16),
            pltpu.VMEM((QR, HEADS * (NOPE + ROPE)), bf16),
            pltpu.VMEM((HEADS, NOPE, LAT), bf16),
            pltpu.VMEM((HEADS, LAT, VD), bf16),
            pltpu.VMEM((GROUP, SIDE), bf16),
            pltpu.VMEM((GROUP, SIDE), bf16),
            pltpu.VMEM((32, KEY, SLAB), bf16),
            pltpu.VMEM((2, HEADS * SLAB, KEY), bf16),
            pltpu.VMEM((2, HEADS * SLAB, LAT), jnp.float32),
            pltpu.VMEM((2, HEADS * SLAB, 128), jnp.float32),
            pltpu.VMEM((2, HEADS * SLAB, 128), jnp.float32),
            pltpu.VMEM((TOK, GROUP), bf16),
            pltpu.VMEM((TOK, GROUP), bf16),
            pltpu.VMEM((14, 2, 32, PAIR), bf16),
            pltpu.VMEM((14, 2, 32, PAIR), bf16),
            pltpu.VMEM((NZ, TOK, WINDOW), jnp.float32),
            dma((7,)),
            dma((N_KV,)),
            dma((N_KV,)),
            dma((9, 4)),
            dma((9, 4)),
            dma((2,)),
            dma((2,)),
            dma((14, 2)),
            dma((14, 2)),
        ],
        compiler_params=pltpu.CompilerParams(
            collective_id=0, has_side_effects=True, vmem_limit_bytes=58 * 2**20
        ),
        name="attention",
    )(c_query, w_uq, w_uk, w_uv, w_out, kv_latent.T, slab_order, block_table)


def solution(mesh):
    in_specs = (
        P("ctx", None),
        P(None, "tp"),
        P("tp", None, None),
        P("tp", None, None),
        P("tp", None),
        P("ctx", None),
        P(),
        P(),
    )
    return jax.shard_map(
        shards, mesh=mesh, in_specs=in_specs, out_specs=P("ctx", "tp"), check_vma=False
    )
```
